32 devices in a mesh: ctx: 8 (over z, x), head: 4 (over y, core).
Axes of the slice: x: 2, y: 2, z: 4, core: 2. Of those that a mesh axis runs over, the one named last changes fastest.
Arguments:
- queries: bfloat16 [8192, 1024], P('ctx', 'head'), may hold values from -6 to 6
- keys: bfloat16 [8192, 1024], P('ctx', 'head'), may hold values from -6 to 6
- values: bfloat16 [8192, 1024], P('ctx', 'head'), may hold values from -6 to 6
- level_index: int32 [8192], P('ctx'), may hold values from 0 to 15
- level_table: float32 [16, 8, 8], P(None, 'head'), may hold values from 0.2 to 2
- head_gain: float32 [1024], P('head'), may hold values from 0.5 to 1.5
- residual: bfloat16 [8192, 1024], P(('ctx', 'head')), may hold values from -6 to 6
- w_out: bfloat16 [1024, 1024], replicated, may hold values from -0.1875 to 0.1875
- norm_gain: float32 [1024], replicated, may hold values from 0.5 to 1.5
- w_qkv: bfloat16 [1024, 3072], replicated, may hold values from -8 to 8
- windows: int32 [8], replicated, may hold values from 64 to 256, as said below
Outputs:
- hidden: bfloat16 [8192, 1024], P(('ctx', 'head'))
- attended: bfloat16 [8192, 1024], P('ctx', 'head')
The draws below stay inside these ranges and needn't reach their ends.
Inputs may be any that keep to these rules, and one draw needn't show every extreme that they name: `windows`: each head's key window; some head's window is exactly 256 in every draw.
All inputs are finite; a program needn't handle non-finite values.
Results may differ from the reference program's by a relative error of at most 0.014.
Values may be sent and summed in bfloat16 or wider, within the bound.
A program may use at most 128 MiB of HBM per device.

```python
import math
import jax
import jax.numpy as jnp
from jax import lax

D = 1024
H = 8
DH = 128
STRETCH = 64
WINDOW = 256
NTAB = 16
TOK_DEV = 1024
TOKENS = 8192
LEVELS = 8
N_CTX = 8


def draw_windows(key, part):
    first_key, second_key = jax.random.split(jax.random.fold_in(key, 11))
    drawn = jax.random.randint(first_key, (H,), WINDOW // 4, WINDOW + 1, dtype=jnp.int32)
    chosen = jax.random.randint(second_key, (), 0, H, dtype=jnp.int32)
    return jnp.where(jnp.arange(H, dtype=jnp.int32) == chosen, WINDOW, drawn).astype(jnp.int32)


def draw_w_qkv(key, part):
    base_key = jax.random.fold_in(jax.random.fold_in(key, 23), 0)
    base = jax.random.normal(base_key, (D, 3, H, DH), jnp.float32) * D ** (-0.5)
    return jnp.clip(base, -8.0, 8.0).reshape(D, 3 * D).astype(jnp.bfloat16)


def set_ends(values, own_key, low, high):
    shape = values.shape
    place = [jax.random.randint(jax.random.fold_in(own_key, axis), (), 0, shape[axis]) for axis in range(len(shape))]
    values = values.at[tuple(place)].set(low)
    longest = shape.index(max(shape))
    place[longest] = (place[longest] + 1) % shape[longest]
    return values.at[tuple(place)].set(high)


def steps_of(stream_key, extent, pieces, smallest, high):
    level, own = 1.0, jax.random.fold_in(stream_key, 6)
    for position, parts in pieces:
        steps = jnp.exp(jax.random.uniform(jax.random.fold_in(own, position), (parts,), jnp.float32, smallest / len(pieces), high / len(pieces)))
        level = level * jnp.repeat(steps, extent[position] // parts).reshape([-1 if axis == position else 1 for axis in range(len(extent))])
    return level


def normal_values(rng, shape, deviation, bound, cuts=(), held_as=jnp.bfloat16):
    values = deviation * jax.random.normal(rng, shape, jnp.float32)
    if cuts:
        values = values * steps_of(rng, shape, cuts, -0.22, 0.18)
    return jnp.clip(values, -bound, bound).astype(held_as)


def setup_inputs(seed: int = 0) -> dict:
    key_list = jax.random.split(jax.random.key(seed), 12)
    queries = normal_values(key_list[0], (TOKENS, D), 1.0, 6.0, ((0, 8), (1, 4)))
    keys = normal_values(key_list[1], (TOKENS, D), 1.0, 6.0, ((0, 8), (1, 4)))
    values = normal_values(key_list[2], (TOKENS, D), 1.0, 6.0, ((0, 8), (1, 4)))
    level_index = set_ends(jax.random.randint(key_list[3], (TOKENS,), 0, NTAB), jax.random.fold_in(key_list[3], 1), 0, NTAB - 1).astype(jnp.int32)
    level_table = jnp.clip(jnp.exp(math.log(2.0) - 2.3025851 * jax.random.uniform(key_list[4], (NTAB, H, LEVELS), jnp.float32) ** steps_of(key_list[4], (NTAB, H, LEVELS), ((1, 4),), -0.2, 0.2)), 0.2, 2.0)
    head_gain = jnp.clip(1.0 + 0.1 * jax.random.normal(key_list[5], (D,), jnp.float32), 0.5, 1.5)
    residual = normal_values(key_list[6], (TOKENS, D), 1.0, 6.0, ((0, 32),))
    w_out = normal_values(key_list[7], (D, D), D ** -0.5, 0.1875)
    norm_gain = jnp.clip(1.0 + 0.1 * jax.random.normal(key_list[8], (D,), jnp.float32), 0.5, 1.5)
    w_qkv = draw_w_qkv(jax.random.fold_in(key_list[11], 71), 0)
    windows = draw_windows(jax.random.fold_in(key_list[11], 71), 0)
    return {"queries": queries, "keys": keys, "values": values, "level_index": level_index, "level_table": level_table, "head_gain": head_gain, "residual": residual, "w_out": w_out, "norm_gain": norm_gain, "w_qkv": w_qkv, "windows": windows}


EPSILON = 1e-05
PRECISE = lax.Precision.HIGHEST

def rounded(array):
    return lax.optimization_barrier(array.astype(jnp.bfloat16)).astype(jnp.float32)

def reference(queries, keys, values, level_index, level_table, head_gain, residual, w_out, norm_gain, w_qkv, windows):
    stretch_count = TOKENS // STRETCH
    bit_count = LEVELS - 1
    query_all = queries.reshape(stretch_count, STRETCH, H, DH)
    key_all = keys.reshape(stretch_count, STRETCH, H, DH)
    value_all = values.reshape(stretch_count, STRETCH, H, DH)
    level_weight = level_table[level_index].reshape(stretch_count, STRETCH, H, LEVELS)
    level_rates = jnp.array([STRETCH ** (-0.5)] + [(STRETCH * 2 ** level_bit) ** (-0.5) for level_bit in range(bit_count)], jnp.float32)
    causal = jnp.arange(STRETCH, dtype=jnp.int32)[:, None] >= jnp.arange(STRETCH, dtype=jnp.int32)[None, :]
    bit_numbers = jnp.arange(bit_count, dtype=jnp.int32)
    spans = 2 ** bit_numbers

    def advance(carry, inputs):
        partial_sums, finished = carry
        stretch_index, query_stretch, key_stretch, value_stretch, weight_stretch = inputs
        query_f = query_stretch.astype(jnp.float32)
        key_f = key_stretch.astype(jnp.float32)
        value_f = value_stretch.astype(jnp.float32)
        scores = jnp.einsum('thd,shd->hts', query_f, key_f)
        scores = rounded(jnp.where(causal[None], scores, 0.0))
        inside = jnp.einsum('hts,shd->thd', scores, value_f)
        combined = weight_stretch[:, :, 0][:, :, None] * level_rates[0] * inside
        active = (stretch_index // spans % 2).astype(jnp.float32)
        read_state = rounded(finished) * active[:, None, None, None]
        far_terms = jnp.einsum('thd,bhde->tbhe', query_f, read_state, precision=PRECISE)
        combined = combined + jnp.einsum('tbhe,thb->the', far_terms, weight_stretch[:, :, 1:] * level_rates[1:], precision=PRECISE)
        stretch_state = jnp.einsum('thd,the->hde', key_f, value_f, precision=PRECISE)
        partial_sums = partial_sums + stretch_state[None]
        closing = (stretch_index + 1) % spans == 0
        finished = jnp.where(closing[:, None, None, None], partial_sums, finished)
        partial_sums = jnp.where(closing[:, None, None, None], 0.0, partial_sums)
        return ((partial_sums, finished), combined)
    empty_states = jnp.zeros((bit_count, H, DH, DH), jnp.float32)
    stretch_ids = jnp.arange(stretch_count, dtype=jnp.int32)
    carry_out, heads_raw = lax.scan(advance, (empty_states, empty_states), (stretch_ids, query_all, key_all, value_all, level_weight))
    heads_raw = heads_raw.reshape(TOKENS, H, DH)
    mean_square = lax.optimization_barrier(jnp.mean(heads_raw * heads_raw, -1, keepdims=True))
    heads_out = (heads_raw * lax.rsqrt(mean_square + EPSILON) * head_gain.reshape(H, DH)).astype(jnp.bfloat16).reshape(TOKENS, D)
    projected = jnp.dot(heads_out, w_out, preferred_element_type=jnp.float32)
    hidden = (residual.astype(jnp.float32) + projected).astype(jnp.bfloat16)
    hidden_f = hidden.astype(jnp.float32)
    normed = (hidden_f * lax.rsqrt(lax.optimization_barrier(jnp.mean(hidden_f * hidden_f, -1, keepdims=True)) + EPSILON) * norm_gain).astype(jnp.bfloat16)
    projected_qkv = jnp.dot(normed, w_qkv, preferred_element_type=jnp.float32).astype(jnp.bfloat16).reshape(TOKENS, 3, H, DH)
    padding = jnp.zeros((WINDOW, H, DH), jnp.bfloat16)
    query_rows = projected_qkv[:, 0]
    key_padded = jnp.concatenate([padding, projected_qkv[:, 1]], 0)
    value_padded = jnp.concatenate([padding, projected_qkv[:, 2]], 0)

    def attend(start):
        query_block = lax.dynamic_slice_in_dim(query_rows, start, TOK_DEV, 0).astype(jnp.float32)
        key_block = lax.dynamic_slice_in_dim(key_padded, start, TOK_DEV + WINDOW, 0).astype(jnp.float32)
        value_block = lax.dynamic_slice_in_dim(value_padded, start, TOK_DEV + WINDOW, 0).astype(jnp.float32)
        scores = jnp.einsum('qhd,khd->hqk', query_block, key_block) * DH ** (-0.5)
        query_pos = start + jnp.arange(TOK_DEV, dtype=jnp.int32)
        key_pos = start - WINDOW + jnp.arange(TOK_DEV + WINDOW, dtype=jnp.int32)
        distance = query_pos[:, None] - key_pos[None, :]
        allowed = (distance >= 0)[None] & (distance < windows[:, None, None]) & (key_pos >= 0)[None, None, :]
        scores = jnp.where(allowed, scores, -1e+30)
        row_max = lax.optimization_barrier(jnp.max(scores, -1, keepdims=True))
        weights = jnp.exp(scores - row_max)
        probs = rounded(weights / lax.optimization_barrier(jnp.sum(weights, -1, keepdims=True)))
        block_out = jnp.einsum('hqk,khd->qhd', probs, value_block)
        return block_out.astype(jnp.bfloat16).reshape(TOK_DEV, D)
    starts = jnp.arange(N_CTX, dtype=jnp.int32) * TOK_DEV
    attended = lax.map(attend, starts).reshape(TOKENS, D)
    return (hidden, attended)
```

```python
import functools
import math

import jax
import jax.numpy as jnp
from jax import lax
from jax.experimental import pallas as pl
from jax.experimental.pallas import tpu as pltpu
from jax.sharding import PartitionSpec as P

STRETCH = 64
EPSILON = 1e-05
MESH = pl.DeviceIdType.MESH
F32 = jnp.float32
BF16 = jnp.bfloat16


def dot(a, b):
    return jnp.dot(a, b, preferred_element_type=F32)


def dot_tn(a, b):
    return lax.dot_general(a, b, (((0,), (0,)), ((), ())), preferred_element_type=F32)


def dot_nt(a, b):
    return lax.dot_general(a, b, (((1,), (1,)), ((), ())), preferred_element_type=F32)


def kernel(
    n_ctx,
    group,
    local_heads,
    q_hbm,
    k_hbm,
    v_hbm,
    index_ref,
    table_ref,
    head_gain_ref,
    res_hbm,
    w_out_hbm,
    norm_gain_ref,
    w_qkv_hbm,
    windows_ref,
    hidden_ref,
    attended_ref,
    q_ref,
    k_ref,
    v_ref,
    res_ref,
    ho_ref,
    w_out_ref,
    w_qkv_ref,
    acc_ref,
    read_ref,
    cur_ref,
    state_send,
    state_recv,
    spread_ref,
    qs_ref,
    kv_ref,
    local_sem,
    st_send_sem,
    st_recv_sem,
    res_send_sem,
    res_recv_sem,
    ho_send_sem,
    ho_recv_sem,
    halo_send_sem,
    halo_recv_sem,
):
    tokens, width = q_ref.shape
    dim = width // local_heads
    rows = tokens // group
    model = w_out_ref.shape[1]
    ctx_bits = n_ctx.bit_length() - 1
    chunk_bits = group.bit_length() - 1
    inner = rows // STRETCH
    inner_bits = inner.bit_length() - 1
    levels = 1 + inner_bits + chunk_bits + ctx_bits
    ntab = table_ref.shape[0]
    hops = group // 2 - 1

    pos = lax.axis_index("ctx")
    me = lax.axis_index("head")
    sib = me + 1 - 2 * lax.rem(me, 2)

    def ahead(j):
        return lax.rem(me + 2 * j, group)

    def behind(j):
        return lax.rem(me + group - 2 * j, group)

    def bit_of(b):
        return lax.rem(pos // (2**b), 2)

    def partner(b):
        return pos + 2**b - 2 ** (b + 1) * bit_of(b)

    loads = []

    def load(src, dst):
        copy = pltpu.make_async_copy(src, dst, local_sem.at[len(loads)])
        copy.start()
        loads.append(copy)
        return copy

    load_k = load(k_hbm, k_ref)
    load_v = load(v_hbm, v_ref)
    load_q = load(q_hbm, q_ref)
    load_res = load(res_hbm, res_ref.at[me])
    load_wo = load(w_out_hbm, w_out_ref)
    load_w3 = [
        load(
            w_qkv_hbm.at[:, pl.ds(pl.multiple_of(s * model + me * width, width), width)],
            w_qkv_ref.at[:, pl.ds(s * width, width)],
        )
        for s in range(3)
    ]

    barrier = pltpu.get_barrier_semaphore()
    pl.semaphore_signal(barrier, inc=1, device_id={"head": sib}, device_id_type=MESH)
    for j in range(1, hops + 1):
        pl.semaphore_signal(barrier, inc=1, device_id={"head": ahead(j)}, device_id_type=MESH)
    for b in range(ctx_bits):
        pl.semaphore_signal(barrier, inc=1, device_id={"ctx": partner(b)}, device_id_type=MESH)

    @pl.when(pos > 0)
    def _():
        pl.semaphore_signal(barrier, inc=1, device_id={"ctx": pos - 1}, device_id_type=MESH)

    @pl.when(pos < n_ctx - 1)
    def _():
        pl.semaphore_signal(barrier, inc=1, device_id={"ctx": pos + 1}, device_id_type=MESH)

    neighbours = jnp.minimum(pos, 1) + jnp.minimum(n_ctx - 1 - pos, 1)
    pl.semaphore_wait(barrier, 1 + hops + ctx_bits + neighbours)

    def remote(src, dst, send, recv, where):
        return pltpu.make_async_remote_copy(
            src_ref=src,
            dst_ref=dst,
            send_sem=send,
            recv_sem=recv,
            device_id=where,
            device_id_type=MESH,
        )

    def res_copy(slot, source, to):
        src = res_hbm if slot <= hops else res_ref.at[source]
        return remote(
            src, res_ref.at[source], res_send_sem.at[slot], res_recv_sem.at[slot], {"head": to}
        )

    def ho_copy(slot, c, source, to):
        block = ho_ref.at[source, c]
        return remote(
            block, block, ho_send_sem.at[slot, c], ho_recv_sem.at[slot, c], {"head": to}
        )

    def state_copy(b):
        return remote(
            state_send.at[b],
            state_recv.at[b],
            st_send_sem.at[b],
            st_recv_sem.at[b],
            {"ctx": partner(b)},
        )

    def halo_copy():
        return remote(
            kv_ref.at[group],
            kv_ref.at[0],
            halo_send_sem,
            halo_recv_sem,
            {"ctx": jnp.minimum(pos + 1, n_ctx - 1)},
        )

    def state_start(b):
        state_send[b] = cur_ref[...].astype(BF16)
        state_copy(b).start()

    def state_finish(b):
        state_copy(b).wait_recv()
        arrived = state_recv[b]
        used = jnp.where(bit_of(b) == 1, arrived, jnp.zeros_like(arrived))
        for h in range(local_heads):
            read_ref[h, :, b * dim : (b + 1) * dim] = used[h * dim : (h + 1) * dim]
        cur_ref[...] += arrived.astype(F32)

    load_k.wait()
    load_v.wait()
    states = []
    for h in range(local_heads):
        cols = slice(h * dim, (h + 1) * dim)
        mine = [
            dot_tn(k_ref[c * rows : (c + 1) * rows, cols], v_ref[c * rows : (c + 1) * rows, cols])
            for c in range(group)
        ]
        states.append(mine)
        cur_ref[cols, :] = functools.reduce(lambda a, b: a + b, mine)
    state_start(0)
    res_copy(0, me, sib).start()
    for j in range(1, hops + 1):
        res_copy(j, me, ahead(j)).start()

    for h in range(local_heads):
        for level in range(levels):
            column = h * levels + level
            rate = (STRETCH * 2 ** max(level - 1, 0)) ** (-0.5)
            full = jnp.broadcast_to(table_ref[:, column : column + 1] * rate, (ntab, dim))
            high = full.astype(BF16)
            rest = full - high.astype(F32)
            mid = rest.astype(BF16)
            low = (rest - mid.astype(F32)).astype(BF16)
            spread_ref[:, column * dim : (column + 1) * dim] = jnp.concatenate([high, mid, low], 0)

    entry = lax.broadcasted_iota(jnp.int32, (3 * ntab, rows), 0)
    entry = lax.rem(entry, ntab)

    def weights(offset, h, first, count):
        chosen = jnp.broadcast_to(index_ref[:, pl.ds(offset, rows)], (3 * ntab, rows))
        onehot = (chosen == entry).astype(F32).astype(BF16)
        start = (h * levels + first) * dim
        return dot_tn(onehot, spread_ref[:, start : start + count * dim])

    t = lax.broadcasted_iota(jnp.int32, (rows, rows), 0)
    s = lax.broadcasted_iota(jnp.int32, (rows, rows), 1)
    load_q.wait()

    def near(c):
        offset = c * rows
        span = slice(offset, offset + rows)
        tc = t // STRETCH
        sc = s // STRETCH
        for h in range(local_heads):
            cols = slice(h * dim, (h + 1) * dim)
            w = weights(offset, h, 0, 1 + inner_bits + chunk_bits)

            def wide(level):
                return jnp.concatenate([w[:, level * dim : (level + 1) * dim]] * (rows // dim), 1)

            q = q_ref[span, cols]
            scores = dot_nt(q, k_ref[span, cols])
            factor = jnp.where((tc == sc) & (s <= t), wide(0), 0.0)
            for b in range(inner_bits):
                member = (sc // 2**b) == (tc // 2**b) - 1
                member &= lax.rem(tc // 2**b, 2) == 1
                factor = jnp.where(member, wide(1 + b), factor)
            out = dot((scores * factor).astype(BF16), v_ref[span, cols])
            for b in range(chunk_bits):
                first = (c >> (b + 1)) << (b + 1)
                last = (c >> b) << b
                if last > first:
                    bucket = functools.reduce(lambda x, y: x + y, states[h][first:last])
                    level = 1 + inner_bits + b
                    out += w[:, level * dim : (level + 1) * dim] * dot(q, bucket.astype(BF16))
            acc_ref[span, cols] = out

    for i in range(group):
        near(group - 1 - i)
        if i < ctx_bits - 1:
            state_finish(i)
            state_start(i + 1)
    for b in range(min(group, ctx_bits - 1), ctx_bits):
        state_finish(b)
        if b < ctx_bits - 1:
            state_start(b + 1)

    def far(i, carry):
        c = group - 1 - i
        offset = pl.multiple_of(c * rows, rows)
        span = pl.ds(offset, rows)
        for h in range(local_heads):
            cols = slice(h * dim, (h + 1) * dim)
            w = weights(offset, h, 1 + inner_bits + chunk_bits, ctx_bits)
            part = w * dot(q_ref[span, cols], read_ref[h])
            out = acc_ref[span, cols]
            for b in range(ctx_bits):
                out += part[:, b * dim : (b + 1) * dim]
            square = jnp.mean(out * out, -1, keepdims=True)
            out = out * lax.rsqrt(square + EPSILON) * head_gain_ref[:, cols]
            ho_ref[me, c, :, cols] = out.astype(BF16)
        for j in range(1, hops + 1):
            ho_copy(j, c, me, ahead(j)).start()
        ho_copy(0, c, me, sib).start()
        return carry

    lax.fori_loop(0, group, far, 0)

    load_res.wait()
    for j in range(1, hops + 1):
        res_copy(j, behind(j), me).wait_recv()
        res_copy(hops + j, behind(j), sib).start()
    load_wo.wait()
    for copy in load_w3:
        copy.wait()

    def forward(c):
        for j in range(1, hops + 1):
            ho_copy(j, c, behind(j), me).wait_recv()
            ho_copy(hops + j, c, behind(j), sib).start()

    def forwarded(j):
        return lax.rem(sib + group - 2 * j, group)

    forward(group - 1)
    res_copy(0, sib, me).wait_recv()
    for j in range(1, hops + 1):
        res_copy(hops + j, forwarded(j), me).wait_recv()

    score_scale = dim ** (-0.5) * math.log2(math.e)

    def attend(c, first):
        offset = c * rows
        if not isinstance(c, int):
            offset = pl.multiple_of(offset, rows)
        for h in range(local_heads):
            cols = slice(h * dim, (h + 1) * dim)
            window = windows_ref[me * local_heads + h]
            before = jnp.where(pos == 0, 0, window) if first else window
            q = qs_ref[c, :, cols]
            distance = t - s
            old = dot_nt(q, kv_ref[c, 0, :, cols]) * score_scale
            new = dot_nt(q, kv_ref[c + 1, 0, :, cols]) * score_scale
            old = jnp.where(distance + rows < before, old, -1e30)
            new = jnp.where((distance >= 0) & (distance < window), new, -1e30)
            top = jnp.max(jnp.maximum(old, new), -1, keepdims=True)
            old = jnp.exp2(old - top)
            new = jnp.exp2(new - top)
            total = jnp.sum(old + new, -1, keepdims=True)
            out = dot(old.astype(BF16), kv_ref[c, 1, :, cols])
            out += dot(new.astype(BF16), kv_ref[c + 1, 1, :, cols])
            attended_ref[pl.ds(offset, rows), cols] = (out * (1.0 / total)).astype(BF16)

    def project(i, carry):
        c = group - 1 - i
        ho_copy(0, c, sib, me).wait_recv()
        for j in range(1, hops + 1):
            ho_copy(hops + j, c, forwarded(j), me).wait_recv()
        heads = jnp.concatenate([ho_ref[g, c] for g in range(group)], 1)
        hidden = (res_ref[c].astype(F32) + dot(heads, w_out_ref[...])).astype(BF16)

        @pl.when(c == me)
        def _():
            hidden_ref[...] = hidden

        hidden = hidden.astype(F32)
        square = jnp.mean(hidden * hidden, -1, keepdims=True)
        normed = (hidden * lax.rsqrt(square + EPSILON) * norm_gain_ref[...]).astype(BF16)
        qkv = dot(normed, w_qkv_ref[...]).astype(BF16)
        qs_ref[c] = qkv[:, :width]
        kv_ref[c + 1, 0] = qkv[:, width : 2 * width]
        kv_ref[c + 1, 1] = qkv[:, 2 * width :]

        @pl.when((i == 0) & (pos < n_ctx - 1))
        def _():
            halo_copy().start()

        @pl.when(i < group - 1)
        def _():
            forward(c - 1)

        @pl.when(i > 0)
        def _():
            attend(c + 1, False)

        return carry

    lax.fori_loop(0, group, project, 0)

    @pl.when(pos > 0)
    def _():
        halo_copy().wait_recv()

    @pl.when(pos == 0)
    def _():
        kv_ref[0] = jnp.zeros(kv_ref.shape[1:], BF16)

    attend(0, True)

    @pl.when(pos < n_ctx - 1)
    def _():
        halo_copy().wait_send()

    for b in range(ctx_bits):
        state_copy(b).wait_send()
    res_copy(0, me, sib).wait_send()
    for j in range(1, hops + 1):
        res_copy(j, me, ahead(j)).wait_send()
        res_copy(hops + j, behind(j), sib).wait_send()
    for c in range(group):
        ho_copy(0, c, me, sib).wait_send()
        for j in range(1, hops + 1):
            ho_copy(j, c, me, ahead(j)).wait_send()
            ho_copy(hops + j, c, behind(j), sib).wait_send()


def per_device(
    n_ctx,
    group,
    queries,
    keys,
    values,
    level_index,
    level_table,
    head_gain,
    residual,
    w_out,
    norm_gain,
    w_qkv,
    windows,
):
    tokens, width = queries.shape
    ntab, local_heads, levels = level_table.shape
    dim = width // local_heads
    rows = tokens // group
    model = w_out.shape[1]
    ctx_bits = n_ctx.bit_length() - 1
    slots = 1 + 2 * (group // 2 - 1)
    vmem = pl.BlockSpec(memory_space=pltpu.VMEM)
    smem = pl.BlockSpec(memory_space=pltpu.SMEM)
    anywhere = pl.BlockSpec(memory_space=pl.ANY)
    dma = pltpu.SemaphoreType.DMA
    call = pl.pallas_call(
        functools.partial(kernel, n_ctx, group, local_heads),
        out_shape=(
            jax.ShapeDtypeStruct(residual.shape, BF16),
            jax.ShapeDtypeStruct(queries.shape, BF16),
        ),
        in_specs=[
            anywhere,
            anywhere,
            anywhere,
            vmem,
            vmem,
            vmem,
            anywhere,
            anywhere,
            vmem,
            anywhere,
            smem,
        ],
        out_specs=(vmem, vmem),
        scratch_shapes=[
            pltpu.VMEM((tokens, width), BF16),
            pltpu.VMEM((tokens, width), BF16),
            pltpu.VMEM((tokens, width), BF16),
            pltpu.VMEM((group, rows, model), BF16),
            pltpu.VMEM((group, group, rows, width), BF16),
            pltpu.VMEM(w_out.shape, BF16),
            pltpu.VMEM((model, 3 * width), BF16),
            pltpu.VMEM((tokens, width), F32),
            pltpu.VMEM((local_heads, dim, ctx_bits * dim), BF16),
            pltpu.VMEM((width, dim), F32),
            pltpu.VMEM((ctx_bits, width, dim), BF16),
            pltpu.VMEM((ctx_bits, width, dim), BF16),
            pltpu.VMEM((3 * ntab, local_heads * levels * dim), BF16),
            pltpu.VMEM((group, rows, width), BF16),
            pltpu.VMEM((group + 1, 2, rows, width), BF16),
            dma((8,)),
            dma((ctx_bits,)),
            dma((ctx_bits,)),
            dma((slots,)),
            dma((slots,)),
            dma((slots, group)),
            dma((slots, group)),
            dma,
            dma,
        ],
        compiler_params=pltpu.CompilerParams(
            collective_id=0, has_side_effects=True, vmem_limit_bytes=48 * 2**20
        ),
    )
    return call(
        queries,
        keys,
        values,
        level_index.reshape(1, tokens),
        level_table.reshape(ntab, local_heads * levels),
        head_gain.reshape(1, width),
        residual,
        w_out,
        norm_gain.reshape(1, model),
        w_qkv,
        windows,
    )


def solution(mesh):
    in_specs = (
        P("ctx", "head"),
        P("ctx", "head"),
        P("ctx", "head"),
        P("ctx"),
        P(None, "head", None),
        P("head"),
        P(("ctx", "head"), None),
        P(),
        P(),
        P(),
        P(),
    )
    out_specs = (P(("ctx", "head"), None), P("ctx", "head"))
    return jax.shard_map(
        functools.partial(per_device, mesh.shape["ctx"], mesh.shape["head"]),
        mesh=mesh,
        in_specs=in_specs,
        out_specs=out_specs,
        check_vma=False,
    )
```

```python
import functools
import math

import jax
import jax.numpy as jnp
from jax import lax
from jax.experimental import pallas as pl
from jax.experimental.pallas import tpu as pltpu
from jax.sharding import PartitionSpec as P

STRETCH = 64
EPSILON = 1e-05
VMEM_BYTES = 60 * 2**20
MESH = pl.DeviceIdType.MESH
F32 = jnp.float32
BF16 = jnp.bfloat16


def dot(a, b):
    return jnp.dot(a, b, preferred_element_type=F32)


def dot_tn(a, b):
    return lax.dot_general(a, b, (((0,), (0,)), ((), ())), preferred_element_type=F32)


def dot_nt(a, b):
    return lax.dot_general(a, b, (((1,), (1,)), ((), ())), preferred_element_type=F32)


def kernel(
    n_ctx,
    group,
    local_heads,
    q_hbm,
    k_hbm,
    v_hbm,
    index_hbm,
    table_hbm,
    head_gain_hbm,
    res_hbm,
    w_out_hbm,
    norm_gain_hbm,
    w_qkv_hbm,
    windows_hbm,
    hidden_ref,
    attended_ref,
    q_ref,
    k_ref,
    v_ref,
    res_ref,
    ho_ref,
    w_out_ref,
    w_qkv_ref,
    acc_ref,
    read_ref,
    cur_ref,
    state_send,
    state_recv,
    spread_ref,
    qs_ref,
    kv_ref,
    index_ref,
    table_ref,
    head_gain_ref,
    norm_gain_ref,
    windows_ref,
    local_sem,
    st_send_sem,
    st_recv_sem,
    res_send_sem,
    res_recv_sem,
    ho_send_sem,
    ho_recv_sem,
    halo_send_sem,
    halo_recv_sem,
):
    tokens, width = q_ref.shape
    dim = width // local_heads
    rows = tokens // group
    model = w_out_ref.shape[1]
    ctx_bits = n_ctx.bit_length() - 1
    chunk_bits = group.bit_length() - 1
    inner = rows // STRETCH
    inner_bits = inner.bit_length() - 1
    levels = 1 + inner_bits + chunk_bits + ctx_bits
    ntab = table_ref.shape[1]
    hops = group // 2 - 1

    pos = lax.axis_index("ctx")
    me = lax.axis_index("head")
    sib = me + 1 - 2 * lax.rem(me, 2)

    def ahead(j):
        return lax.rem(me + 2 * j, group)

    def behind(j):
        return lax.rem(me + group - 2 * j, group)

    def bit_of(b):
        return lax.rem(pos // (2**b), 2)

    def partner(b):
        return pos + 2**b - 2 ** (b + 1) * bit_of(b)

    loads = []

    def load(src, dst):
        copy = pltpu.make_async_copy(src, dst, local_sem.at[len(loads)])
        copy.start()
        loads.append(copy)
        return copy

    load_k = load(k_hbm, k_ref)
    load_v = load(v_hbm, v_ref)
    small = [
        load(table_hbm, table_ref),
        load(index_hbm, index_ref),
        load(head_gain_hbm, head_gain_ref),
        load(norm_gain_hbm, norm_gain_ref),
        load(windows_hbm, windows_ref),
    ]
    load_q = load(q_hbm, q_ref)
    load_res = load(res_hbm, res_ref.at[me])
    load_wo = load(w_out_hbm, w_out_ref)
    load_w3 = [
        load(
            w_qkv_hbm.at[:, pl.ds(pl.multiple_of(s * model + me * width, width), width)],
            w_qkv_ref.at[:, pl.ds(s * width, width)],
        )
        for s in range(3)
    ]

    barrier = pltpu.get_barrier_semaphore()
    pl.semaphore_signal(barrier, inc=1, device_id={"head": sib}, device_id_type=MESH)
    for j in range(1, hops + 1):
        pl.semaphore_signal(barrier, inc=1, device_id={"head": ahead(j)}, device_id_type=MESH)
    for b in range(ctx_bits):
        pl.semaphore_signal(barrier, inc=1, device_id={"ctx": partner(b)}, device_id_type=MESH)

    @pl.when(pos > 0)
    def _():
        pl.semaphore_signal(barrier, inc=1, device_id={"ctx": pos - 1}, device_id_type=MESH)

    @pl.when(pos < n_ctx - 1)
    def _():
        pl.semaphore_signal(barrier, inc=1, device_id={"ctx": pos + 1}, device_id_type=MESH)

    neighbours = jnp.minimum(pos, 1) + jnp.minimum(n_ctx - 1 - pos, 1)
    pl.semaphore_wait(barrier, 1 + hops + ctx_bits + neighbours)

    def remote(src, dst, send, recv, where):
        return pltpu.make_async_remote_copy(
            src_ref=src,
            dst_ref=dst,
            send_sem=send,
            recv_sem=recv,
            device_id=where,
            device_id_type=MESH,
        )

    def res_copy(slot, source, to):
        src = res_hbm if slot <= hops else res_ref.at[source]
        return remote(
            src, res_ref.at[source], res_send_sem.at[slot], res_recv_sem.at[slot], {"head": to}
        )

    def ho_copy(slot, c, source, to):
        block = ho_ref.at[source, c]
        return remote(
            block, block, ho_send_sem.at[slot, c], ho_recv_sem.at[slot, c], {"head": to}
        )

    def state_copy(b):
        return remote(
            state_send.at[b],
            state_recv.at[b],
            st_send_sem.at[b],
            st_recv_sem.at[b],
            {"ctx": partner(b)},
        )

    def halo_copy():
        return remote(
            kv_ref.at[group],
            kv_ref.at[0],
            halo_send_sem,
            halo_recv_sem,
            {"ctx": jnp.minimum(pos + 1, n_ctx - 1)},
        )

    def state_start(b):
        state_send[b] = cur_ref[...].astype(BF16)
        state_copy(b).start()

    def state_finish(b):
        state_copy(b).wait_recv()
        arrived = state_recv[b]
        used = jnp.where(bit_of(b) == 1, arrived, jnp.zeros_like(arrived))
        for h in range(local_heads):
            read_ref[h, :, b * dim : (b + 1) * dim] = used[h * dim : (h + 1) * dim]
        cur_ref[...] += arrived.astype(F32)

    load_k.wait()
    load_v.wait()
    states = []
    for h in range(local_heads):
        cols = slice(h * dim, (h + 1) * dim)
        mine = [
            dot_tn(k_ref[c * rows : (c + 1) * rows, cols], v_ref[c * rows : (c + 1) * rows, cols])
            for c in range(group)
        ]
        states.append(mine)
        cur_ref[cols, :] = functools.reduce(lambda a, b: a + b, mine)
    state_start(0)
    res_copy(0, me, sib).start()
    for j in range(1, hops + 1):
        res_copy(j, me, ahead(j)).start()

    for copy in small:
        copy.wait()
    columns = local_heads * levels
    place = lax.broadcasted_iota(jnp.int32, (columns, 1), 0)
    level = lax.rem(place, levels)
    rate = jnp.full((columns, 1), STRETCH ** (-0.5), F32)
    for b in range(1, levels - 1):
        rate = jnp.where(level == b + 1, (STRETCH * 2**b) ** (-0.5), rate)
    full = table_ref[...] * rate
    high = full.astype(BF16)
    rest = full - high.astype(F32)
    mid = rest.astype(BF16)
    low = (rest - mid.astype(F32)).astype(BF16)
    row = lax.broadcasted_iota(jnp.int32, (columns, columns * dim), 0)
    lane = lax.broadcasted_iota(jnp.int32, (columns, columns * dim), 1)
    spread = (lane // dim == row).astype(F32).astype(BF16)
    for i, term in enumerate((high, mid, low)):
        spread_ref[i * ntab : (i + 1) * ntab] = dot_tn(term, spread).astype(BF16)

    entry = lax.broadcasted_iota(jnp.int32, (3 * ntab, rows), 0)
    entry = lax.rem(entry, ntab)

    def weights(offset, h, first, count):
        chosen = jnp.broadcast_to(index_ref[:, pl.ds(offset, rows)], (3 * ntab, rows))
        onehot = (chosen == entry).astype(F32).astype(BF16)
        start = (h * levels + first) * dim
        return dot_tn(onehot, spread_ref[:, start : start + count * dim])

    t = lax.broadcasted_iota(jnp.int32, (rows, rows), 0)
    s = lax.broadcasted_iota(jnp.int32, (rows, rows), 1)
    load_q.wait()

    def near(c):
        offset = c * rows
        span = slice(offset, offset + rows)
        tc = t // STRETCH
        sc = s // STRETCH
        for h in range(local_heads):
            cols = slice(h * dim, (h + 1) * dim)
            w = weights(offset, h, 0, 1 + inner_bits + chunk_bits)

            def wide(level):
                return jnp.concatenate([w[:, level * dim : (level + 1) * dim]] * (rows // dim), 1)

            q = q_ref[span, cols]
            scores = dot_nt(q, k_ref[span, cols])
            factor = jnp.where((tc == sc) & (s <= t), wide(0), 0.0)
            for b in range(inner_bits):
                member = (sc // 2**b) == (tc // 2**b) - 1
                member &= lax.rem(tc // 2**b, 2) == 1
                factor = jnp.where(member, wide(1 + b), factor)
            out = dot((scores * factor).astype(BF16), v_ref[span, cols])
            for b in range(chunk_bits):
                first = (c >> (b + 1)) << (b + 1)
                last = (c >> b) << b
                if last > first:
                    bucket = functools.reduce(lambda x, y: x + y, states[h][first:last])
                    level = 1 + inner_bits + b
                    out += w[:, level * dim : (level + 1) * dim] * dot(q, bucket.astype(BF16))
            acc_ref[span, cols] = out

    for i in range(group):
        near(group - 1 - i)
        if i < ctx_bits - 1:
            state_finish(i)
            state_start(i + 1)
    for b in range(min(group, ctx_bits - 1), ctx_bits):
        state_finish(b)
        if b < ctx_bits - 1:
            state_start(b + 1)

    def far(i, carry):
        c = group - 1 - i
        offset = pl.multiple_of(c * rows, rows)
        span = pl.ds(offset, rows)
        for h in range(local_heads):
            cols = slice(h * dim, (h + 1) * dim)
            w = weights(offset, h, 1 + inner_bits + chunk_bits, ctx_bits)
            part = w * dot(q_ref[span, cols], read_ref[h])
            out = acc_ref[span, cols]
            for b in range(ctx_bits):
                out += part[:, b * dim : (b + 1) * dim]
            square = jnp.mean(out * out, -1, keepdims=True)
            out = out * lax.rsqrt(square + EPSILON) * head_gain_ref[:, cols]
            ho_ref[me, c, :, cols] = out.astype(BF16)
        for j in range(1, hops + 1):
            ho_copy(j, c, me, ahead(j)).start()
        ho_copy(0, c, me, sib).start()
        return carry

    lax.fori_loop(0, group, far, 0)

    load_res.wait()
    for j in range(1, hops + 1):
        res_copy(j, behind(j), me).wait_recv()
        res_copy(hops + j, behind(j), sib).start()
    load_wo.wait()
    for copy in load_w3:
        copy.wait()

    def forward(c):
        for j in range(1, hops + 1):
            ho_copy(j, c, behind(j), me).wait_recv()
            ho_copy(hops + j, c, behind(j), sib).start()

    def forwarded(j):
        return lax.rem(sib + group - 2 * j, group)

    forward(group - 1)
    res_copy(0, sib, me).wait_recv()
    for j in range(1, hops + 1):
        res_copy(hops + j, forwarded(j), me).wait_recv()

    score_scale = dim ** (-0.5) * math.log2(math.e)

    def attend(c, first):
        offset = c * rows
        if not isinstance(c, int):
            offset = pl.multiple_of(offset, rows)
        for h in range(local_heads):
            cols = slice(h * dim, (h + 1) * dim)
            window = windows_ref[me * local_heads + h]
            before = jnp.where(pos == 0, 0, window) if first else window
            q = qs_ref[c, :, cols]
            distance = t - s
            old = dot_nt(q, kv_ref[c, 0, :, cols]) * score_scale
            new = dot_nt(q, kv_ref[c + 1, 0, :, cols]) * score_scale
            old = jnp.where(distance + rows < before, old, -1e30)
            new = jnp.where((distance >= 0) & (distance < window), new, -1e30)
            top = jnp.max(jnp.maximum(old, new), -1, keepdims=True)
            old = jnp.exp2(old - top)
            new = jnp.exp2(new - top)
            total = jnp.sum(old + new, -1, keepdims=True)
            out = dot(old.astype(BF16), kv_ref[c, 1, :, cols])
            out += dot(new.astype(BF16), kv_ref[c + 1, 1, :, cols])
            attended_ref[pl.ds(offset, rows), cols] = (out * (1.0 / total)).astype(BF16)

    def project(i, carry):
        c = group - 1 - i
        ho_copy(0, c, sib, me).wait_recv()
        for j in range(1, hops + 1):
            ho_copy(hops + j, c, forwarded(j), me).wait_recv()
        heads = jnp.concatenate([ho_ref[g, c] for g in range(group)], 1)
        hidden = (res_ref[c].astype(F32) + dot(heads, w_out_ref[...])).astype(BF16)

        @pl.when(c == me)
        def _():
            hidden_ref[...] = hidden

        hidden = hidden.astype(F32)
        square = jnp.mean(hidden * hidden, -1, keepdims=True)
        normed = (hidden * lax.rsqrt(square + EPSILON) * norm_gain_ref[...]).astype(BF16)
        qkv = dot(normed, w_qkv_ref[...]).astype(BF16)
        qs_ref[c] = qkv[:, :width]
        kv_ref[c + 1, 0] = qkv[:, width : 2 * width]
        kv_ref[c + 1, 1] = qkv[:, 2 * width :]

        @pl.when((i == 0) & (pos < n_ctx - 1))
        def _():
            halo_copy().start()

        @pl.when(i < group - 1)
        def _():
            forward(c - 1)

        @pl.when(i > 0)
        def _():
            attend(c + 1, False)

        return carry

    lax.fori_loop(0, group, project, 0)

    @pl.when(pos > 0)
    def _():
        halo_copy().wait_recv()

    @pl.when(pos == 0)
    def _():
        kv_ref[0] = jnp.zeros(kv_ref.shape[1:], BF16)

    attend(0, True)

    @pl.when(pos < n_ctx - 1)
    def _():
        halo_copy().wait_send()

    for b in range(ctx_bits):
        state_copy(b).wait_send()
    res_copy(0, me, sib).wait_send()
    for j in range(1, hops + 1):
        res_copy(j, me, ahead(j)).wait_send()
        res_copy(hops + j, behind(j), sib).wait_send()
    for c in range(group):
        ho_copy(0, c, me, sib).wait_send()
        for j in range(1, hops + 1):
            ho_copy(j, c, me, ahead(j)).wait_send()
            ho_copy(hops + j, c, behind(j), sib).wait_send()


def per_device(
    n_ctx,
    group,
    queries,
    keys,
    values,
    level_index,
    level_table,
    head_gain,
    residual,
    w_out,
    norm_gain,
    w_qkv,
    windows,
):
    tokens, width = queries.shape
    ntab, local_heads, levels = level_table.shape
    dim = width // local_heads
    rows = tokens // group
    model = w_out.shape[1]
    ctx_bits = n_ctx.bit_length() - 1
    slots = 1 + 2 * (group // 2 - 1)
    vmem = pl.BlockSpec(memory_space=pltpu.VMEM)
    anywhere = pl.BlockSpec(memory_space=pl.ANY)
    dma = pltpu.SemaphoreType.DMA
    call = pl.pallas_call(
        functools.partial(kernel, n_ctx, group, local_heads),
        out_shape=(
            jax.ShapeDtypeStruct(residual.shape, BF16),
            jax.ShapeDtypeStruct(queries.shape, BF16),
        ),
        in_specs=[anywhere] * 11,
        out_specs=(vmem, vmem),
        scratch_shapes=[
            pltpu.VMEM((tokens, width), BF16),
            pltpu.VMEM((tokens, width), BF16),
            pltpu.VMEM((tokens, width), BF16),
            pltpu.VMEM((group, rows, model), BF16),
            pltpu.VMEM((group, group, rows, width), BF16),
            pltpu.VMEM(w_out.shape, BF16),
            pltpu.VMEM((model, 3 * width), BF16),
            pltpu.VMEM((tokens, width), F32),
            pltpu.VMEM((local_heads, dim, ctx_bits * dim), BF16),
            pltpu.VMEM((width, dim), F32),
            pltpu.VMEM((ctx_bits, width, dim), BF16),
            pltpu.VMEM((ctx_bits, width, dim), BF16),
            pltpu.VMEM((3 * ntab, local_heads * levels * dim), BF16),
            pltpu.VMEM((group, rows, width), BF16),
            pltpu.VMEM((group + 1, 2, rows, width), BF16),
            pltpu.VMEM((1, tokens), jnp.int32),
            pltpu.VMEM((local_heads * levels, ntab), F32),
            pltpu.VMEM((1, width), F32),
            pltpu.VMEM((1, model), F32),
            pltpu.SMEM(windows.shape, jnp.int32),
            dma((13,)),
            dma((ctx_bits,)),
            dma((ctx_bits,)),
            dma((slots,)),
            dma((slots,)),
            dma((slots, group)),
            dma((slots, group)),
            dma,
            dma,
        ],
        compiler_params=pltpu.CompilerParams(
            collective_id=0, has_side_effects=True, vmem_limit_bytes=VMEM_BYTES
        ),
    )
    return call(
        queries,
        keys,
        values,
        level_index.reshape(1, tokens),
        level_table.transpose(1, 2, 0).reshape(local_heads * levels, ntab),
        head_gain.reshape(1, width),
        residual,
        w_out,
        norm_gain.reshape(1, model),
        w_qkv,
        windows,
    )


def solution(mesh):
    in_specs = (
        P("ctx", "head"),
        P("ctx", "head"),
        P("ctx", "head"),
        P("ctx"),
        P(None, "head", None),
        P("head"),
        P(("ctx", "head"), None),
        P(),
        P(),
        P(),
        P(),
    )
    out_specs = (P(("ctx", "head"), None), P("ctx", "head"))
    return jax.shard_map(
        functools.partial(per_device, mesh.shape["ctx"], mesh.shape["head"]),
        mesh=mesh,
        in_specs=in_specs,
        out_specs=out_specs,
        check_vma=False,
    )
```

```python
import functools
import math

import jax
import jax.numpy as jnp
from jax import lax
from jax.experimental import pallas as pl
from jax.experimental.pallas import tpu as pltpu
from jax.sharding import PartitionSpec as P

STRETCH = 64
STRETCH_BITS = 6
PIECES = 4
EPSILON = 1e-05
VMEM_BYTES = 60 * 2**20
MESH = pl.DeviceIdType.MESH
F32 = jnp.float32
BF16 = jnp.bfloat16


def dot(a, b):
    return jnp.dot(a, b, preferred_element_type=F32)


def dot_tn(a, b):
    return lax.dot_general(a, b, (((0,), (0,)), ((), ())), preferred_element_type=F32)


def dot_nt(a, b):
    return lax.dot_general(a, b, (((1,), (1,)), ((), ())), preferred_element_type=F32)


def kernel(
    n_ctx,
    group,
    local_heads,
    q_hbm,
    k_hbm,
    v_hbm,
    index_hbm,
    table_hbm,
    head_gain_hbm,
    res_hbm,
    w_out_hbm,
    norm_gain_hbm,
    w_qkv_hbm,
    windows_hbm,
    hidden_ref,
    attended_ref,
    q_ref,
    k_ref,
    v_ref,
    res_ref,
    ho_ref,
    w_out_ref,
    w_qkv_ref,
    acc_ref,
    read_ref,
    cur_ref,
    state_send,
    state_recv,
    spread_ref,
    qs_ref,
    kv_ref,
    index_ref,
    table_ref,
    head_gain_ref,
    norm_gain_ref,
    windows_ref,
    local_sem,
    st_send_sem,
    st_recv_sem,
    res_send_sem,
    res_recv_sem,
    ho_send_sem,
    ho_recv_sem,
    halo_send_sem,
    halo_recv_sem,
):
    tokens, width = q_ref.shape
    dim = width // local_heads
    rows = tokens // group
    model = w_out_ref.shape[1]
    ctx_bits = n_ctx.bit_length() - 1
    chunk_bits = group.bit_length() - 1
    inner = rows // STRETCH
    inner_bits = inner.bit_length() - 1
    levels = 1 + inner_bits + chunk_bits + ctx_bits
    ntab = table_ref.shape[1]
    hops = group // 2 - 1

    pos = lax.axis_index("ctx")
    me = lax.axis_index("head")
    sib = me + 1 - 2 * lax.rem(me, 2)

    def ahead(j):
        return lax.rem(me + 2 * j, group)

    def behind(j):
        return lax.rem(me + group - 2 * j, group)

    def bit_of(b):
        return lax.rem(pos // (2**b), 2)

    def partner(b):
        return pos + 2**b - 2 ** (b + 1) * bit_of(b)

    loads = []

    def load(src, dst):
        copy = pltpu.make_async_copy(src, dst, local_sem.at[len(loads)])
        copy.start()
        loads.append(copy)
        return copy

    load_k = load(k_hbm, k_ref)
    load_v = load(v_hbm, v_ref)
    small = [
        load(table_hbm, table_ref),
        load(index_hbm, index_ref),
        load(head_gain_hbm, head_gain_ref),
        load(norm_gain_hbm, norm_gain_ref),
        load(windows_hbm, windows_ref),
    ]
    load_q = load(q_hbm, q_ref)
    load_res = load(res_hbm, res_ref.at[me])
    load_wo = load(w_out_hbm, w_out_ref)
    load_w3 = [
        load(
            w_qkv_hbm.at[:, pl.ds(pl.multiple_of(s * model + me * width, width), width)],
            w_qkv_ref.at[:, pl.ds(s * width, width)],
        )
        for s in range(3)
    ]

    barrier = pltpu.get_barrier_semaphore()
    pl.semaphore_signal(barrier, inc=1, device_id={"head": sib}, device_id_type=MESH)
    for j in range(1, hops + 1):
        pl.semaphore_signal(barrier, inc=1, device_id={"head": ahead(j)}, device_id_type=MESH)
    for b in range(ctx_bits):
        pl.semaphore_signal(barrier, inc=1, device_id={"ctx": partner(b)}, device_id_type=MESH)

    @pl.when(pos > 0)
    def _():
        pl.semaphore_signal(barrier, inc=1, device_id={"ctx": pos - 1}, device_id_type=MESH)

    @pl.when(pos < n_ctx - 1)
    def _():
        pl.semaphore_signal(barrier, inc=1, device_id={"ctx": pos + 1}, device_id_type=MESH)

    neighbours = jnp.minimum(pos, 1) + jnp.minimum(n_ctx - 1 - pos, 1)
    pl.semaphore_wait(barrier, 1 + hops + ctx_bits + neighbours)

    def remote(src, dst, send, recv, where):
        return pltpu.make_async_remote_copy(
            src_ref=src,
            dst_ref=dst,
            send_sem=send,
            recv_sem=recv,
            device_id=where,
            device_id_type=MESH,
        )

    def res_copy(slot, p, source, to):
        part = pl.ds(p * (rows // PIECES), rows // PIECES)
        src = res_hbm.at[part] if slot <= hops else res_ref.at[source, part]
        return remote(
            src,
            res_ref.at[source, part],
            res_send_sem.at[slot, p],
            res_recv_sem.at[slot, p],
            {"head": to},
        )

    def res_forward(p):
        for j in range(1, hops + 1):
            res_copy(j, p, behind(j), me).wait_recv()
            res_copy(hops + j, p, behind(j), sib).start()

    def ho_copy(slot, c, source, to):
        block = ho_ref.at[source, c]
        return remote(
            block, block, ho_send_sem.at[slot, c], ho_recv_sem.at[slot, c], {"head": to}
        )

    def state_copy(b):
        return remote(
            state_send.at[b],
            state_recv.at[b],
            st_send_sem.at[b],
            st_recv_sem.at[b],
            {"ctx": partner(b)},
        )

    def halo_copy():
        return remote(
            kv_ref.at[group],
            kv_ref.at[0],
            halo_send_sem,
            halo_recv_sem,
            {"ctx": jnp.minimum(pos + 1, n_ctx - 1)},
        )

    def state_start(b):
        state_send[b] = cur_ref[...].astype(BF16)
        state_copy(b).start()

    def state_finish(b):
        state_copy(b).wait_recv()
        arrived = state_recv[b]
        used = jnp.where(bit_of(b) == 1, arrived, jnp.zeros_like(arrived))
        for h in range(local_heads):
            read_ref[h, :, b * dim : (b + 1) * dim] = used[h * dim : (h + 1) * dim]
        cur_ref[...] += arrived.astype(F32)

    for p in range(PIECES):
        for j in range(1, hops + 1):
            res_copy(j, p, me, ahead(j)).start()
        res_copy(0, p, me, sib).start()

    load_k.wait()
    load_v.wait()
    states = []
    for h in range(local_heads):
        cols = slice(h * dim, (h + 1) * dim)
        mine = [
            dot_tn(k_ref[c * rows : (c + 1) * rows, cols], v_ref[c * rows : (c + 1) * rows, cols])
            for c in range(group)
        ]
        states.append(mine)
        cur_ref[cols, :] = functools.reduce(lambda a, b: a + b, mine)
    state_start(0)

    for copy in small:
        copy.wait()
    columns = local_heads * levels
    level = lax.broadcasted_iota(jnp.int32, (columns, 1), 0)
    for h in range(local_heads - 1):
        level = jnp.where(level >= levels, level - levels, level)
    rate = jnp.full((columns, 1), STRETCH ** (-0.5), F32)
    for b in range(1, levels - 1):
        rate = jnp.where(level == b + 1, (STRETCH * 2**b) ** (-0.5), rate)
    full = table_ref[...] * rate
    high = full.astype(BF16)
    rest = full - high.astype(F32)
    mid = rest.astype(BF16)
    low = (rest - mid.astype(F32)).astype(BF16)
    row = lax.broadcasted_iota(jnp.int32, (columns, columns * dim), 0)
    lane = lax.broadcasted_iota(jnp.int32, (columns, columns * dim), 1)
    spread = ((lane >= row * dim) & (lane < (row + 1) * dim)).astype(F32).astype(BF16)
    for i, term in enumerate((high, mid, low)):
        spread_ref[i * ntab : (i + 1) * ntab] = dot_tn(term, spread).astype(BF16)

    entry = jnp.concatenate([lax.broadcasted_iota(jnp.int32, (ntab, rows), 0)] * 3, 0)

    def weights(offset, h, first, count):
        chosen = jnp.broadcast_to(index_ref[:, pl.ds(offset, rows)], (3 * ntab, rows))
        onehot = (chosen == entry).astype(F32).astype(BF16)
        start = (h * levels + first) * dim
        return dot_tn(onehot, spread_ref[:, start : start + count * dim])

    t = lax.broadcasted_iota(jnp.int32, (rows, rows), 0)
    s = lax.broadcasted_iota(jnp.int32, (rows, rows), 1)
    load_q.wait()

    def near(c):
        offset = c * rows
        span = slice(offset, offset + rows)
        tc = t >> STRETCH_BITS
        sc = s >> STRETCH_BITS
        for h in range(local_heads):
            cols = slice(h * dim, (h + 1) * dim)
            w = weights(offset, h, 0, 1 + inner_bits + chunk_bits)

            def wide(level):
                return jnp.concatenate([w[:, level * dim : (level + 1) * dim]] * (rows // dim), 1)

            q = q_ref[span, cols]
            scores = dot_nt(q, k_ref[span, cols])
            factor = jnp.where((tc == sc) & (s <= t), wide(0), 0.0)
            for b in range(inner_bits):
                member = ((sc >> b) == (tc >> b) - 1) & (((tc >> b) & 1) == 1)
                factor = jnp.where(member, wide(1 + b), factor)
            out = dot((scores * factor).astype(BF16), v_ref[span, cols])
            for b in range(chunk_bits):
                first = (c >> (b + 1)) << (b + 1)
                last = (c >> b) << b
                if last > first:
                    bucket = functools.reduce(lambda x, y: x + y, states[h][first:last])
                    level = 1 + inner_bits + b
                    out += w[:, level * dim : (level + 1) * dim] * dot(q, bucket.astype(BF16))
            acc_ref[span, cols] = out

    for i in range(group):
        near(group - 1 - i)
        if i < ctx_bits - 1:
            state_finish(i)
            state_start(i + 1)
        if 1 <= i < 3:
            res_forward(i - 1)
    for b in range(min(group, ctx_bits - 1), ctx_bits):
        state_finish(b)
        if b < ctx_bits - 1:
            state_start(b + 1)

    def far(i, carry):
        c = group - 1 - i
        offset = pl.multiple_of(c * rows, rows)
        span = pl.ds(offset, rows)
        for h in range(local_heads):
            cols = slice(h * dim, (h + 1) * dim)
            w = weights(offset, h, 1 + inner_bits + chunk_bits, ctx_bits)
            part = w * dot(q_ref[span, cols], read_ref[h])
            out = acc_ref[span, cols]
            for b in range(ctx_bits):
                out += part[:, b * dim : (b + 1) * dim]
            square = jnp.mean(out * out, -1, keepdims=True)
            out = out * lax.rsqrt(square + EPSILON) * head_gain_ref[:, cols]
            ho_ref[me, c, :, cols] = out.astype(BF16)
        for j in range(1, hops + 1):
            ho_copy(j, c, me, ahead(j)).start()
        ho_copy(0, c, me, sib).start()
        return carry

    lax.fori_loop(0, group, far, 0)

    load_res.wait()
    for p in range(max(0, min(group, 3) - 1), PIECES):
        res_forward(p)
    load_wo.wait()
    for copy in load_w3:
        copy.wait()

    def forward(c):
        for j in range(1, hops + 1):
            ho_copy(j, c, behind(j), me).wait_recv()
            ho_copy(hops + j, c, behind(j), sib).start()

    def forwarded(j):
        return lax.rem(sib + group - 2 * j, group)

    forward(group - 1)
    for p in range(PIECES):
        res_copy(0, p, sib, me).wait_recv()
        for j in range(1, hops + 1):
            res_copy(hops + j, p, forwarded(j), me).wait_recv()

    score_scale = dim ** (-0.5) * math.log2(math.e)

    def attend(c, first):
        offset = c * rows
        if not isinstance(c, int):
            offset = pl.multiple_of(offset, rows)
        for h in range(local_heads):
            cols = slice(h * dim, (h + 1) * dim)
            window = windows_ref[me * local_heads + h]
            before = jnp.where(pos == 0, 0, window) if first else window
            q = qs_ref[c, :, cols]
            distance = t - s
            old = dot_nt(q, kv_ref[c, 0, :, cols]) * score_scale
            new = dot_nt(q, kv_ref[c + 1, 0, :, cols]) * score_scale
            old = jnp.where(distance + rows < before, old, -1e30)
            new = jnp.where((distance >= 0) & (distance < window), new, -1e30)
            top = jnp.max(jnp.maximum(old, new), -1, keepdims=True)
            old = jnp.exp2(old - top)
            new = jnp.exp2(new - top)
            total = jnp.sum(old + new, -1, keepdims=True)
            out = dot(old.astype(BF16), kv_ref[c, 1, :, cols])
            out += dot(new.astype(BF16), kv_ref[c + 1, 1, :, cols])
            attended_ref[pl.ds(offset, rows), cols] = (out * (1.0 / total)).astype(BF16)

    def project(i, carry):
        c = group - 1 - i
        ho_copy(0, c, sib, me).wait_recv()
        for j in range(1, hops + 1):
            ho_copy(hops + j, c, forwarded(j), me).wait_recv()
        heads = jnp.concatenate([ho_ref[g, c] for g in range(group)], 1)
        hidden = (res_ref[c].astype(F32) + dot(heads, w_out_ref[...])).astype(BF16)

        @pl.when(c == me)
        def _():
            hidden_ref[...] = hidden

        hidden = hidden.astype(F32)
        square = jnp.mean(hidden * hidden, -1, keepdims=True)
        normed = (hidden * lax.rsqrt(square + EPSILON) * norm_gain_ref[...]).astype(BF16)
        qkv = dot(normed, w_qkv_ref[...]).astype(BF16)
        qs_ref[c] = qkv[:, :width]
        kv_ref[c + 1, 0] = qkv[:, width : 2 * width]
        kv_ref[c + 1, 1] = qkv[:, 2 * width :]

        @pl.when((i == 0) & (pos < n_ctx - 1))
        def _():
            halo_copy().start()

        @pl.when(i < group - 1)
        def _():
            forward(c - 1)

        @pl.when(i > 0)
        def _():
            attend(c + 1, False)

        return carry

    lax.fori_loop(0, group, project, 0)

    @pl.when(pos > 0)
    def _():
        halo_copy().wait_recv()

    @pl.when(pos == 0)
    def _():
        kv_ref[0] = jnp.zeros(kv_ref.shape[1:], BF16)

    attend(0, True)

    @pl.when(pos < n_ctx - 1)
    def _():
        halo_copy().wait_send()

    for b in range(ctx_bits):
        state_copy(b).wait_send()
    for p in range(PIECES):
        res_copy(0, p, me, sib).wait_send()
        for j in range(1, hops + 1):
            res_copy(j, p, me, ahead(j)).wait_send()
            res_copy(hops + j, p, behind(j), sib).wait_send()
    for c in range(group):
        ho_copy(0, c, me, sib).wait_send()
        for j in range(1, hops + 1):
            ho_copy(j, c, me, ahead(j)).wait_send()
            ho_copy(hops + j, c, behind(j), sib).wait_send()


def hand_on(hidden_ref, attended_ref, hidden_out, attended_out, hidden_mid, attended_mid, sems):
    moves = []
    ways = ((hidden_ref, hidden_mid, hidden_out), (attended_ref, attended_mid, attended_out))
    for src, mid, dst in ways:
        part = src.shape[0] // PIECES
        for p in range(PIECES):
            span = pl.ds(p * part, part)
            n = len(moves)
            moves.append(
                (
                    pltpu.make_async_copy(src.at[span], mid.at[span], sems.at[0, n]),
                    pltpu.make_async_copy(mid.at[span], dst.at[span], sems.at[1, n]),
                )
            )
            moves[-1][0].start()
    for first, second in moves:
        first.wait()
        second.start()
    for first, second in moves:
        second.wait()


def per_device(
    n_ctx,
    group,
    queries,
    keys,
    values,
    level_index,
    level_table,
    head_gain,
    residual,
    w_out,
    norm_gain,
    w_qkv,
    windows,
):
    tokens, width = queries.shape
    ntab, local_heads, levels = level_table.shape
    dim = width // local_heads
    rows = tokens // group
    model = w_out.shape[1]
    ctx_bits = n_ctx.bit_length() - 1
    slots = 1 + 2 * (group // 2 - 1)
    vmem = pl.BlockSpec(memory_space=pltpu.VMEM)
    anywhere = pl.BlockSpec(memory_space=pl.ANY)
    dma = pltpu.SemaphoreType.DMA
    call = pl.pallas_call(
        functools.partial(kernel, n_ctx, group, local_heads),
        out_shape=(
            jax.ShapeDtypeStruct(residual.shape, BF16),
            jax.ShapeDtypeStruct(queries.shape, BF16),
        ),
        in_specs=[anywhere] * 11,
        out_specs=(vmem, vmem),
        scratch_shapes=[
            pltpu.VMEM((tokens, width), BF16),
            pltpu.VMEM((tokens, width), BF16),
            pltpu.VMEM((tokens, width), BF16),
            pltpu.VMEM((group, rows, model), BF16),
            pltpu.VMEM((group, group, rows, width), BF16),
            pltpu.VMEM(w_out.shape, BF16),
            pltpu.VMEM((model, 3 * width), BF16),
            pltpu.VMEM((tokens, width), F32),
            pltpu.VMEM((local_heads, dim, ctx_bits * dim), BF16),
            pltpu.VMEM((width, dim), F32),
            pltpu.VMEM((ctx_bits, width, dim), BF16),
            pltpu.VMEM((ctx_bits, width, dim), BF16),
            pltpu.VMEM((3 * ntab, local_heads * levels * dim), BF16),
            pltpu.VMEM((group, rows, width), BF16),
            pltpu.VMEM((group + 1, 2, rows, width), BF16),
            pltpu.VMEM((1, tokens), jnp.int32),
            pltpu.VMEM((local_heads * levels, ntab), F32),
            pltpu.VMEM((1, width), F32),
            pltpu.VMEM((1, model), F32),
            pltpu.SMEM(windows.shape, jnp.int32),
            dma((13,)),
            dma((ctx_bits,)),
            dma((ctx_bits,)),
            dma((slots, PIECES)),
            dma((slots, PIECES)),
            dma((slots, group)),
            dma((slots, group)),
            dma,
            dma,
        ],
        compiler_params=pltpu.CompilerParams(
            collective_id=0, has_side_effects=True, vmem_limit_bytes=VMEM_BYTES
        ),
    )
    hidden, attended = call(
        queries,
        keys,
        values,
        level_index.reshape(1, tokens),
        level_table.transpose(1, 2, 0).reshape(local_heads * levels, ntab),
        head_gain.reshape(1, width),
        residual,
        w_out,
        norm_gain.reshape(1, model),
        w_qkv,
        windows,
    )
    return pl.pallas_call(
        hand_on,
        out_shape=(
            jax.ShapeDtypeStruct(residual.shape, BF16),
            jax.ShapeDtypeStruct(queries.shape, BF16),
        ),
        in_specs=[anywhere] * 2,
        out_specs=(anywhere, anywhere),
        scratch_shapes=[
            pltpu.VMEM(residual.shape, BF16),
            pltpu.VMEM(queries.shape, BF16),
            dma((2, 2 * PIECES)),
        ],
        compiler_params=pltpu.CompilerParams(vmem_limit_bytes=VMEM_BYTES),
    )(hidden, attended)


def solution(mesh):
    in_specs = (
        P("ctx", "head"),
        P("ctx", "head"),
        P("ctx", "head"),
        P("ctx"),
        P(None, "head", None),
        P("head"),
        P(("ctx", "head"), None),
        P(),
        P(),
        P(),
        P(),
    )
    out_specs = (P(("ctx", "head"), None), P("ctx", "head"))
    return jax.shard_map(
        functools.partial(per_device, mesh.shape["ctx"], mesh.shape["head"]),
        mesh=mesh,
        in_specs=in_specs,
        out_specs=out_specs,
        check_vma=False,
    )
```
